32 devices in a mesh: rep: 16 (over z, y, core), grp: 2 (over x).
Axes of the slice: x: 2, y: 2, z: 4, core: 2. Of those that a mesh axis runs over, the one named last changes fastest.
Arguments:
- inputs: bfloat16 [32, 1024, 768], P('rep', 'grp'), may hold values from -6 to 6
- pre_gain: bfloat16 [768], P('grp'), may hold values from 0.25 to 1.75
- w_in: bfloat16 [768, 3328], P('grp'), may hold values from -0.21875 to 0.21875
- w_dt: bfloat16 [768, 24], P('grp'), may hold values from -0.21875 to 0.21875
- conv_w: bfloat16 [4, 1792], P(None, 'grp'), may hold values from -3 to 3
- conv_b: bfloat16 [1792], P('grp'), may hold values from -4 to 4
- dt_bias: bfloat16 [24], P('grp'), may hold values from -4.5 to -3.5
- a_log: bfloat16 [24], P('grp'), as said below
- d_skip: bfloat16 [24], P('grp'), may hold values from 0.5 to 1.5
- norm_gain: bfloat16 [1536], P('grp'), may hold values from 0.25 to 1.75
- w_out: bfloat16 [1536, 768], P('grp'), may hold values from -0.15625 to 0.15625
- cotangent: bfloat16 [32, 1024, 768], P('rep', 'grp'), may hold values from -6 to 6
Outputs:
- output: bfloat16 [32, 1024, 768], P('rep', 'grp')
- d_input: bfloat16 [32, 1024, 768], P('rep', 'grp')
- grad_pre_gain: float32 [768], P('grp')
- grad_w_in: float32 [768, 3328], P('grp')
- grad_w_dt: float32 [768, 24], P('grp')
- grad_conv_w: float32 [4, 1792], P(None, 'grp')
- grad_conv_b: float32 [1792], P('grp')
- grad_dt_bias: float32 [24], P('grp')
- grad_a_log: float32 [24], P('grp')
- grad_d_skip: float32 [24], P('grp')
- grad_norm_gain: float32 [1536], P('grp')
- grad_w_out: float32 [1536, 768], P('grp')
The draws below stay inside these ranges and needn't reach their ends.
Inputs may be any that keep to these rules, and one draw needn't show every extreme that they name: `a_log`: each head's log-rate, independent over heads.
All inputs are finite; a program needn't handle non-finite values.
Results may differ from the reference program's by a relative error of at most 0.0075.
Values may be sent and summed in bfloat16 or wider, within the bound.
A program may use at most 192 MiB of HBM per device.

```python
import math
import jax
import jax.numpy as jnp
from jax import lax

D = 768
E = 1536
H = 24
P_SIZE = 64
N = 128
K = 4
BLOCK = 256
LEN = 1024
BATCH = 32
CH = 1792
PROJ = 3328


def draw_a_log(key, part):
    key = jax.random.fold_in(key, 7)
    lowest = math.log(5.0 / LEN)
    highest = math.log(2.0)
    values = jax.random.uniform(key, (H,), jnp.float32, lowest, highest)
    return values.astype(jnp.bfloat16)


def shard_levels(rng, extent, shards, least, largest):
    def one(dim, shards_of):
        draws = jax.random.uniform(jax.random.fold_in(jax.random.fold_in(rng, 6), dim), (shards_of,), jnp.float32, least / len(shards), largest / len(shards))
        return jnp.repeat(jnp.exp(draws), extent[dim] // shards_of).reshape((-1,) + (1,) * (len(extent) - dim - 1))

    level = one(*shards[0])
    for cut in shards[1:]:
        level = level * one(*cut)
    return level


def scatter_about(own_key, extent, width, limit, pieces=(), kind=jnp.bfloat16):
    values = jax.random.normal(own_key, extent, jnp.float32) * width
    if len(pieces) > 0:
        values = shard_levels(own_key, extent, pieces, -0.22, 0.18) * values
    return jnp.clip(values, min=-limit, max=limit).astype(kind)


def setup_inputs(seed: int = 0) -> dict:
    key_list = jax.random.split(jax.random.key(seed), 13)
    inputs = scatter_about(key_list[0], (BATCH, LEN, D), 1.0, 6.0, ((0, 16), (1, 2)))
    pre_gain = jnp.clip(1.0 + 0.15 * jax.random.normal(key_list[1], (D,), jnp.float32), 0.25, 1.75).astype(jnp.bfloat16)
    w_in = scatter_about(key_list[2], (D, PROJ), D ** -0.5, 0.21875, ((0, 2),))
    w_dt = scatter_about(key_list[3], (D, H), D ** -0.5, 0.21875, ((0, 2),))
    conv_w = scatter_about(key_list[4], (K, CH), K ** -0.5, 3.0, ((1, 2),))
    conv_b = scatter_about(key_list[5], (CH,), 0.3, 4.0, ((0, 2),))
    dt_bias = jnp.clip(-4.5 + 1.0 * jax.random.uniform(key_list[6], (H,), jnp.float32) ** shard_levels(key_list[6], (H,), ((0, 2),), -0.2, 0.2), -4.5, -3.5).astype(jnp.bfloat16)
    a_log = draw_a_log(jax.random.fold_in(key_list[12], 71), 0)
    d_skip = jnp.clip(0.5 + 1.0 * jax.random.uniform(key_list[8], (H,), jnp.float32) ** shard_levels(key_list[8], (H,), ((0, 2),), -0.2, 0.2), 0.5, 1.5).astype(jnp.bfloat16)
    norm_gain = jnp.clip(1.0 + 0.15 * jax.random.normal(key_list[9], (E,), jnp.float32), 0.25, 1.75).astype(jnp.bfloat16)
    w_out = scatter_about(key_list[10], (E, D), E ** -0.5, 0.15625, ((0, 2),))
    cotangent = scatter_about(key_list[11], (BATCH, LEN, D), 1.0, 6.0, ((0, 16), (1, 2)))
    return dict(inputs=inputs, pre_gain=pre_gain, w_in=w_in, w_dt=w_dt, conv_w=conv_w, conv_b=conv_b, dt_bias=dt_bias, a_log=a_log, d_skip=d_skip, norm_gain=norm_gain, w_out=w_out, cotangent=cotangent)


exact_mode = lax.Precision.HIGHEST

@jax.custom_vjp
def low(v):
    return lax.optimization_barrier(v.astype(jnp.bfloat16)).astype(jnp.float32)

@jax.custom_vjp
def low_back(v):
    return v

def low_keep(v):
    return (low(v), None)

def low_pass(kept, grad):
    return (grad,)

def back_keep(v):
    return (v, None)

def back_low(kept, grad):
    return (low(grad),)
low.defvjp(low_keep, low_pass)
low_back.defvjp(back_keep, back_low)

def rms_scale(values, gain_vector):
    return values * lax.rsqrt(lax.optimization_barrier(jnp.mean(values * values, axis=-1, keepdims=True)) + 1e-05) * gain_vector

def block_out(operands):
    heads_x, b_rows, c_rows, step_size, decay_rate, start_state = operands
    cumul = jnp.cumsum(decay_rate, axis=0)
    places = jnp.arange(BLOCK)
    lower_mask = (places[:, None] >= places[None, :]).astype(jnp.float32)
    spread = cumul.T[:, :, None] - cumul.T[:, None, :]
    decays = jnp.exp(spread * lower_mask) * lower_mask
    scores = jnp.dot(c_rows, b_rows.T, precision=exact_mode)
    mixing = scores[None] * decays * step_size.T[:, None, :]
    inner_part = jnp.einsum('hts,shp->thp', mixing, heads_x, precision=exact_mode)
    carried = jnp.einsum('tn,hpn->thp', c_rows, start_state, precision=exact_mode)
    return inner_part + carried * jnp.exp(cumul)[:, :, None]

def advance(state_now, operands):
    heads_x, b_rows, c_rows, step_size, decay_rate = operands
    cumul = jnp.cumsum(decay_rate, axis=0)
    weights_last = jnp.exp(cumul[-1:] - cumul) * step_size
    added = jnp.einsum('qhp,qn->hpn', weights_last[..., None] * heads_x, b_rows, precision=exact_mode)
    new_state = jnp.exp(cumul[-1])[:, None, None] * state_now + added
    return (new_state, block_out((heads_x, b_rows, c_rows, step_size, decay_rate, state_now)))

def layer(seq_in, weight_set):
    pre_gain, w_in, w_dt, conv_w, conv_b, dt_bias, a_log, d_skip, norm_gain, w_out = weight_set
    hidden = low(rms_scale(seq_in, pre_gain))
    projected = low_back(jnp.dot(hidden, w_in, precision=exact_mode))
    dt_linear = low_back(jnp.dot(hidden, w_dt, precision=exact_mode))
    gate_rows = projected[:, :E]
    xbc_rows = projected[:, E:]
    padded = jnp.concatenate([jnp.zeros((K - 1, CH), jnp.float32), xbc_rows], axis=0)
    summed = jnp.zeros_like(xbc_rows) + conv_b
    for offset in range(K):
        summed = summed + conv_w[offset] * padded[offset:offset + LEN]
    mixed_rows = jax.nn.silu(summed)
    blocks = LEN // BLOCK
    heads_x = mixed_rows[:, :E].reshape(blocks, BLOCK, H, P_SIZE)
    b_rows = mixed_rows[:, E:E + N].reshape(blocks, BLOCK, N)
    c_rows = mixed_rows[:, E + N:].reshape(blocks, BLOCK, N)
    step_size = jax.nn.softplus(dt_linear + dt_bias).reshape(blocks, BLOCK, H)
    decay_rate = -step_size * jnp.exp(a_log)
    initial = jnp.zeros((H, P_SIZE, N), jnp.float32)
    _, outputs = lax.scan(jax.checkpoint(advance), initial, (heads_x, b_rows, c_rows, step_size, decay_rate))
    mixed_y = outputs + d_skip[:, None] * heads_x
    gated_rows = mixed_y.reshape(LEN, E) * jax.nn.silu(gate_rows)
    normed = low(rms_scale(gated_rows, norm_gain))
    return seq_in + jnp.dot(normed, w_out, precision=exact_mode)

def reference(inputs, pre_gain, w_in, w_dt, conv_w, conv_b, dt_bias, a_log, d_skip, norm_gain, w_out, cotangent):
    weight_set = tuple((member.astype(jnp.float32) for member in (pre_gain, w_in, w_dt, conv_w, conv_b, dt_bias, a_log, d_skip, norm_gain, w_out)))

    def per_sequence(totals, seq_pair):
        seq_in, seq_cot = seq_pair
        result, pullback = jax.vjp(layer, seq_in.astype(jnp.float32), weight_set)
        d_seq, d_weights = pullback(seq_cot.astype(jnp.float32))
        totals = tuple((running + gradient for running, gradient in zip(totals, d_weights)))
        return (totals, (result.astype(jnp.bfloat16), d_seq.astype(jnp.bfloat16)))
    initial = tuple((jnp.zeros_like(member) for member in weight_set))
    totals, (results, d_inputs) = lax.scan(per_sequence, initial, (inputs, cotangent))
    return (results, d_inputs, totals[0], totals[1], totals[2], totals[3], totals[4], totals[5], totals[6], totals[7], totals[8], totals[9])
```

```python
import jax
import jax.numpy as jnp
from jax import lax
from jax.experimental import pallas as pl
from jax.experimental.pallas import tpu as pltpu
from jax.sharding import PartitionSpec as P

E = 1536
H = 24
P_SIZE = 64
N = 128
K = 4
BLOCK = 256
CH = E + 2 * N
PAD = 128
EPS = 1e-05
FAR = -1e30
SEND = jnp.bfloat16
VMEM = 56 * 1024 * 1024

f32 = jnp.float32
bf16 = jnp.bfloat16


def nn(a, b):
    return lax.dot_general(a, b, (((1,), (0,)), ((), ())), preferred_element_type=f32)


def nt(a, b):
    return lax.dot_general(a, b, (((1,), (1,)), ((), ())), preferred_element_type=f32)


def tn(a, b):
    return lax.dot_general(a, b, (((0,), (0,)), ((), ())), preferred_element_type=f32)


def split2(v):
    hi = v.astype(bf16)
    return hi, (v - hi.astype(f32)).astype(bf16)


def split3(v):
    hi = v.astype(bf16)
    rest = v - hi.astype(f32)
    mid = rest.astype(bf16)
    return hi, mid, (rest - mid.astype(f32)).astype(bf16)


def triangle(lower):
    row = lax.broadcasted_iota(jnp.int32, (BLOCK, BLOCK), 0)
    col = lax.broadcasted_iota(jnp.int32, (BLOCK, BLOCK), 1)
    return row >= col if lower else col >= row


def running_sum(mask, v):
    ones = jnp.where(mask, 1.0, 0.0).astype(bf16)
    hi, mid, lo = split3(v)
    return nn(ones, hi) + nn(ones, mid) + nn(ones, lo)


def spread_heads(v, heads2):
    return nn(jnp.concatenate(split2(v), axis=1), heads2)


def sum_heads(v, heads):
    hi, lo = split2(v)
    return nt(hi, heads) + nt(lo, heads)


def softplus(v):
    return jnp.maximum(v, 0.0) + jnp.log1p(jnp.exp(-jnp.abs(v)))


def sigmoid(v):
    return 1.0 / (1.0 + jnp.exp(-v))


def rates(dt, bias, log_rate):
    step = softplus(dt + bias)
    rate = -step * jnp.exp(log_rate)
    cum = running_sum(triangle(True), rate)
    return step, rate, cum


def conv_sum(ext, conv_w, conv_b):
    summed = conv_b
    for k in range(K):
        summed = summed + conv_w[k : k + 1, :] * ext[5 + k : 5 + k + BLOCK, :]
    return summed


def forward_kernel(
    in_ref, cot_ref, pre_ref, w_in_ref, w_dt_ref, cw_ref, cb_ref, bias_ref, log_ref, skip_ref,
    gain_ref, w_out_ref, heads2_ref,
    hid_o, xbc_o, dt_o, norm_o, dgate_o, dy_o, r1_o, start_o, gain_o, skip_o,
    ext, state, inner,
):
    first = pl.program_id(0) == 0

    @pl.when(first)
    def _():
        ext[0:8, :] = jnp.zeros((8, CH), f32)
        state[...] = jnp.zeros_like(state)
        gain_o[...] = jnp.zeros_like(gain_o)
        skip_o[...] = jnp.zeros_like(skip_o)

    values = in_ref[...].astype(f32)
    scale = lax.rsqrt(jnp.mean(values * values, axis=-1, keepdims=True) + EPS)
    hidden = (values * scale * pre_ref[...]).astype(bf16)
    hid_o[...] = hidden
    xbc = nn(hidden, w_in_ref[:, E:])
    xbc_o[...] = xbc
    ext[8:, :] = xbc
    dt = nn(hidden, w_dt_ref[...])
    dt_o[...] = dt
    step, rate, cum = rates(dt, bias_ref[...], log_ref[...])
    last = cum[BLOCK - 1 : BLOCK, :]
    cum_t = cum.T
    summed = conv_sum(ext, cw_ref[...], cb_ref[...])
    tail = ext[BLOCK : BLOCK + 8, :]
    ext[0:8, :] = tail
    mixed = summed * sigmoid(summed)
    x = mixed[:, :E]
    b = mixed[:, E : E + N].astype(bf16)
    c = mixed[:, E + N :].astype(bf16)
    heads2 = heads2_ref[...]
    xd = (x * spread_heads(step, heads2)).astype(bf16)
    scores = nt(c, b)
    mask = triangle(True)
    low_lane = lax.broadcasted_iota(jnp.int32, (BLOCK, PAD), 1) < P_SIZE
    for pair in range(H // 2):
        lanes = slice(pair * PAD, (pair + 1) * PAD)
        part = xd[:, lanes]
        total = None
        for side in range(2):
            h = 2 * pair + side
            far = jnp.where(mask, cum[:, h : h + 1] - cum_t[h : h + 1, :], FAR)
            mixing = (scores * jnp.exp(far)).astype(bf16)
            keep = low_lane if side == 0 else jnp.logical_not(low_lane)
            one = nn(mixing, jnp.where(keep, part, jnp.zeros_like(part)))
            total = one if total is None else total + one
        inner[:, lanes] = total
    start = state[...].astype(bf16)
    start_o[0] = start
    y_inner = inner[...] + nn(c, start) * spread_heads(jnp.exp(cum), heads2)
    to_last = (xd.astype(f32) * spread_heads(jnp.exp(last - cum), heads2)).astype(bf16)
    whole = spread_heads(jnp.broadcast_to(jnp.exp(last), (8, PAD)), heads2)[0:1, :]
    state[...] = whole * state[...] + tn(b, to_last)

    y = y_inner + skip_ref[...] * x
    gate = nn(hidden, w_in_ref[:, :E])
    sig = sigmoid(gate)
    opened = gate * sig
    gated = y * opened
    out_scale = lax.rsqrt(jnp.mean(gated * gated, axis=-1, keepdims=True) + EPS)
    unit = gated * out_scale
    gain = gain_ref[...]
    norm_o[...] = (unit * gain).astype(bf16)
    d_normed = nt(cot_ref[...], w_out_ref[...])
    gain_o[...] += jnp.sum(d_normed * unit, axis=0, keepdims=True)
    d_unit = d_normed * gain
    d_gated = out_scale * (d_unit - unit * jnp.mean(d_unit * unit, axis=-1, keepdims=True))
    dy = d_gated * opened
    dgate_o[...] = (d_gated * y * (sig + opened * (1.0 - sig))).astype(bf16)
    dy_low = dy.astype(bf16)
    dy_o[...] = dy_low
    r1_o[...] = sum_heads(dy_low.astype(f32) * y_inner, heads2[:PAD, :])
    skip_o[...] += jnp.sum(dy * x, axis=0, keepdims=True)


def backward_kernel(
    xbc_ref, before_ref, dt_ref, dy_ref, r1_ref, start_ref, cw_ref, cb_ref, bias_ref, log_ref,
    skip_ref, heads2_ref,
    dxbc_o, ddt_o, gcw_o, gcb_o, gbias_o, glog_o,
    ext, ext_back, d_state, d_inner, d_scores,
):
    step_id = pl.program_id(0)
    steps = pl.num_programs(0)

    @pl.when(step_id == 0)
    def _():
        ext_back[BLOCK:, :] = jnp.zeros((8, CH), f32)
        d_state[...] = jnp.zeros_like(d_state)
        gcw_o[...] = jnp.zeros_like(gcw_o)
        gcb_o[...] = jnp.zeros_like(gcb_o)
        gbias_o[...] = jnp.zeros_like(gbias_o)
        glog_o[...] = jnp.zeros_like(glog_o)

    xbc = xbc_ref[...]
    ext[0:8, :] = jnp.where(step_id == steps - 1, 0.0, before_ref[...])
    ext[8:, :] = xbc
    cw = cw_ref[...]
    summed = conv_sum(ext, cw, cb_ref[...])
    sig = sigmoid(summed)
    mixed = summed * sig
    d_silu = sig + mixed * (1.0 - sig)
    x = mixed[:, :E]
    b = mixed[:, E : E + N].astype(bf16)
    c = mixed[:, E + N :].astype(bf16)
    dt = dt_ref[...]
    step, rate, cum = rates(dt, bias_ref[...], log_ref[...])
    last = cum[BLOCK - 1 : BLOCK, :]
    cum_t = cum.T
    heads2 = heads2_ref[...]
    heads = heads2[:PAD, :]
    step_e = spread_heads(step, heads2)
    xd = (x * step_e).astype(bf16)
    dy = dy_ref[...]
    scores_t = nt(b, c)
    mask = triangle(False)
    low_lane = lax.broadcasted_iota(jnp.int32, (BLOCK, PAD), 1) < P_SIZE
    d_scores[...] = jnp.zeros_like(d_scores)
    for pair in range(H // 2):
        lanes = slice(pair * PAD, (pair + 1) * PAD)
        part = xd[:, lanes]
        dpart = dy[:, lanes]
        total = None
        for side in range(2):
            h = 2 * pair + side
            far = jnp.where(mask, cum_t[h : h + 1, :] - cum[:, h : h + 1], FAR)
            decay = jnp.exp(far)
            mixing = (scores_t * decay).astype(bf16)
            keep = low_lane if side == 0 else jnp.logical_not(low_lane)
            d_scores[...] += nt(jnp.where(keep, part, jnp.zeros_like(part)), dpart) * decay
            one = nn(mixing, jnp.where(keep, dpart, jnp.zeros_like(dpart)))
            total = one if total is None else total + one
        d_inner[:, lanes] = total
    start = start_ref[0]
    d_last = d_state[...]
    d_last_low = d_last.astype(bf16)
    to_last = spread_heads(jnp.exp(last - cum), heads2)
    carried = to_last * nn(b, d_last_low)
    dxd = d_inner[...] + carried
    xd32 = xd.astype(f32)
    whole = spread_heads(jnp.broadcast_to(jnp.exp(last), (8, PAD)), heads2)[0:1, :]
    end_row = jnp.sum(xd32 * carried, axis=0, keepdims=True) + whole * jnp.sum(
        d_last * start.astype(f32), axis=0, keepdims=True
    )
    r3 = sum_heads(jnp.broadcast_to(end_row, (8, E)), heads)[0:1, :]
    row = lax.broadcasted_iota(jnp.int32, (BLOCK, PAD), 0)
    d_cum = r1_ref[...] - sum_heads(xd32 * dxd, heads) + jnp.where(row == BLOCK - 1, r3, 0.0)
    d_rate = running_sum(triangle(False), d_cum)
    d_step = sum_heads(dxd * x, heads) - jnp.exp(log_ref[...]) * d_rate
    glog_o[...] += jnp.sum(d_rate * rate, axis=0, keepdims=True)
    ddt = d_step * sigmoid(dt + bias_ref[...])
    gbias_o[...] += jnp.sum(ddt, axis=0, keepdims=True)
    ddt_o[...] = ddt.astype(bf16)
    dy32 = dy.astype(f32)
    dx = dxd * step_e + skip_ref[...] * dy32
    dy_e = (dy32 * spread_heads(jnp.exp(cum), heads2)).astype(bf16)
    weighted = (xd32 * to_last).astype(bf16)
    d_sc = d_scores[...].astype(bf16)
    d_c = tn(d_sc, b) + nt(dy_e, start)
    d_b = nn(d_sc, c) + nt(weighted, d_last_low)
    d_state[...] = whole * d_last + tn(c, dy_e)
    d_sum = jnp.concatenate([dx, d_b, d_c], axis=1) * d_silu
    gcb_o[...] += jnp.sum(d_sum, axis=0, keepdims=True)
    ext_back[0:BLOCK, :] = d_sum
    total = None
    for k in range(K):
        later = ext_back[K - 1 - k : K - 1 - k + BLOCK, :]
        gcw_o[k : k + 1, :] += jnp.sum(xbc * later, axis=0, keepdims=True)
        one = cw[k : k + 1, :] * later
        total = one if total is None else total + one
    dxbc_o[...] = total.astype(bf16)
    head = ext_back[0:8, :]
    ext_back[BLOCK:, :] = head


def whole_spec(shape):
    return pl.BlockSpec(shape, lambda i: tuple(0 for _ in shape))


def forward_call(seq, cot, pre, w_in, w_dt, cw, cb, bias, log_rate, skip, gain, w_out, heads2):
    tokens, width = seq.shape
    blocks = tokens // BLOCK
    rows = lambda n: pl.BlockSpec((BLOCK, n), lambda i: (i, 0))
    out = jax.ShapeDtypeStruct
    weights = (pre, w_in, w_dt, cw, cb, bias, log_rate, skip, gain, w_out, heads2)
    return pl.pallas_call(
        forward_kernel,
        grid=(blocks,),
        in_specs=[rows(width), rows(width)] + [whole_spec(w.shape) for w in weights],
        out_specs=[
            rows(width), rows(CH), rows(PAD), rows(E), rows(E), rows(E), rows(PAD),
            pl.BlockSpec((1, N, E), lambda i: (i, 0, 0)),
            whole_spec((1, E)), whole_spec((1, E)),
        ],
        out_shape=[
            out((tokens, width), bf16), out((tokens, CH), f32), out((tokens, PAD), f32),
            out((tokens, E), bf16), out((tokens, E), bf16), out((tokens, E), bf16),
            out((tokens, PAD), f32), out((blocks, N, E), bf16), out((1, E), f32), out((1, E), f32),
        ],
        scratch_shapes=[
            pltpu.VMEM((BLOCK + 8, CH), f32), pltpu.VMEM((N, E), f32), pltpu.VMEM((BLOCK, E), f32),
        ],
        compiler_params=pltpu.CompilerParams(vmem_limit_bytes=VMEM),
        cost_estimate=pl.CostEstimate(
            flops=20_000_000_000, bytes_accessed=40_000_000, transcendentals=12_000_000
        ),
        name="mixer_forward",
    )(seq, cot, *weights)


def backward_call(xbc, dt, dy, r1, starts, cw, cb, bias, log_rate, skip, heads2):
    tokens = xbc.shape[0]
    blocks = tokens // BLOCK
    per = BLOCK // 8
    rows = lambda n: pl.BlockSpec((BLOCK, n), lambda i: (blocks - 1 - i, 0))
    out = jax.ShapeDtypeStruct
    weights = (cw, cb, bias, log_rate, skip, heads2)
    return pl.pallas_call(
        backward_kernel,
        grid=(blocks,),
        in_specs=[
            rows(CH),
            pl.BlockSpec((8, CH), lambda i: (jnp.maximum((blocks - 1 - i) * per - 1, 0), 0)),
            rows(PAD), rows(E), rows(PAD),
            pl.BlockSpec((1, N, E), lambda i: (blocks - 1 - i, 0, 0)),
        ]
        + [whole_spec(w.shape) for w in weights],
        out_specs=[
            rows(CH), rows(PAD), whole_spec((K, CH)), whole_spec((1, CH)), whole_spec((1, PAD)),
            whole_spec((1, PAD)),
        ],
        out_shape=[
            out((tokens, CH), bf16), out((tokens, PAD), bf16), out((K, CH), f32),
            out((1, CH), f32), out((1, PAD), f32), out((1, PAD), f32),
        ],
        scratch_shapes=[
            pltpu.VMEM((BLOCK + 8, CH), f32), pltpu.VMEM((BLOCK + 8, CH), f32),
            pltpu.VMEM((N, E), f32), pltpu.VMEM((BLOCK, E), f32), pltpu.VMEM((BLOCK, BLOCK), f32),
        ],
        compiler_params=pltpu.CompilerParams(vmem_limit_bytes=VMEM),
        cost_estimate=pl.CostEstimate(
            flops=20_000_000_000, bytes_accessed=30_000_000, transcendentals=12_000_000
        ),
        name="mixer_backward",
    )(xbc, xbc, dt, dy, r1, starts, *weights)


SWAP = [(0, 1), (1, 0)]


def to_sequence(pieces, mine):
    kept = lax.dynamic_index_in_dim(pieces, mine, 0, keepdims=False)
    other = lax.ppermute(lax.dynamic_index_in_dim(pieces, 1 - mine, 0, keepdims=False), "grp", SWAP)
    early = jnp.where(mine == 0, kept, other)
    late = jnp.where(mine == 0, other, kept)
    return jnp.concatenate([early, late], axis=0)


def to_pieces(seq, mine):
    halves = seq.reshape(2, seq.shape[0] // 2, seq.shape[1])
    kept = lax.dynamic_index_in_dim(halves, mine, 0, keepdims=False)
    other = lax.ppermute(lax.dynamic_index_in_dim(halves, 1 - mine, 0, keepdims=False), "grp", SWAP)
    return jnp.where(mine == 0, jnp.stack([kept, other]), jnp.stack([other, kept]))


def pad_heads(v):
    return jnp.pad(v, [(0, 0)] * (v.ndim - 1) + [(0, PAD - H)])


def reduced(grad):
    part = lax.psum_scatter(grad.astype(SEND), "grp", scatter_dimension=0, tiled=True)
    return lax.psum(part, "rep").astype(f32)


def per_device(
    inputs, pre_gain, w_in, w_dt, conv_w, conv_b, dt_bias, a_log, d_skip, norm_gain, w_out,
    cotangent,
):
    mine = lax.axis_index("grp")
    gather = lambda v, axis=0: lax.all_gather(v, "grp", axis=axis, tiled=True)
    vectors = jnp.concatenate(
        [conv_w.reshape(-1), pre_gain, conv_b, dt_bias, a_log, d_skip, norm_gain, w_dt.reshape(-1)]
    )
    both = lax.all_gather(vectors, "grp", axis=0)
    sizes = [conv_w.size, pre_gain.size, conv_b.size, H // 2, H // 2, H // 2, norm_gain.size]
    cuts, at = [], 0
    for size in sizes:
        cuts.append(both[:, at : at + size])
        at += size
    half = conv_w.shape[1]
    cw = cuts[0].reshape(2, K, half).transpose(1, 0, 2).reshape(K, CH).astype(f32)
    pre, cb, bias, log_rate, skip, gain = (v.reshape(1, -1).astype(f32) for v in cuts[1:])
    wdt = pad_heads(both[:, at:].reshape(-1, H))
    bias, log_rate = pad_heads(bias), pad_heads(log_rate)
    skip = jnp.repeat(skip, P_SIZE, axis=1)
    win = gather(w_in)
    wout = gather(w_out)
    heads = (jnp.arange(PAD)[:, None] == jnp.arange(E)[None, :] // P_SIZE).astype(bf16)
    heads2 = jnp.concatenate([heads, heads], axis=0)
    seq = to_sequence(inputs, mine)
    cot = to_sequence(cotangent, mine)
    hidden, xbc, dt, normed, d_gate, dy, r1, starts, g_gain, g_skip = forward_call(
        seq, cot, pre, win, wdt, cw, cb, bias, log_rate, skip, gain, wout, heads2
    )
    grad_out_w = reduced(tn(normed, cot))
    grad_gate_w = reduced(tn(hidden, d_gate))
    result = to_pieces((seq.astype(f32) + nn(normed, wout)).astype(bf16), mine)
    d_xbc, d_dt, g_cw, g_cb, g_bias, g_log = backward_call(
        xbc, dt, dy, r1, starts, cw, cb, bias, log_rate, skip, heads2
    )
    grad_xbc_w = reduced(tn(hidden, d_xbc))
    grad_in_w = jnp.concatenate([grad_gate_w, grad_xbc_w], axis=1)
    d_hidden = nt(d_gate, win[:, :E]) + nt(d_xbc, win[:, E:]) + nt(d_dt, wdt)
    seq32 = seq.astype(f32)
    scale = lax.rsqrt(jnp.mean(seq32 * seq32, axis=-1, keepdims=True) + EPS)
    unit = seq32 * scale
    g_pre = jnp.sum(d_hidden * unit, axis=0)
    d_unit = d_hidden * pre
    d_seq = scale * (d_unit - unit * jnp.mean(d_unit * unit, axis=-1, keepdims=True))
    d_inputs = to_pieces((cot.astype(f32) + d_seq).astype(bf16), mine)
    g_wdt = tn(hidden, d_dt)[:, :H]
    g_skip_h = g_skip.reshape(H, P_SIZE).sum(axis=1)
    small = jnp.concatenate(
        [
            g_wdt.reshape(2, -1), g_pre.reshape(2, -1),
            g_cw.reshape(K, 2, half).transpose(1, 0, 2).reshape(2, -1), g_cb.reshape(2, -1),
            g_gain.reshape(2, -1), g_bias[0, :H].reshape(2, -1), g_log[0, :H].reshape(2, -1),
            g_skip_h.reshape(2, -1),
        ],
        axis=1,
    )
    small = lax.psum(small, ("rep", "grp"))
    small = lax.dynamic_index_in_dim(small, mine, 0, keepdims=False)
    parts, at = [], 0
    for size in (w_dt.size, pre_gain.size, conv_w.size, half, norm_gain.size, 12, 12, 12):
        parts.append(small[at : at + size])
        at += size
    return (
        result, d_inputs, parts[1], grad_in_w, parts[0].reshape(w_dt.shape),
        parts[2].reshape(K, half), parts[3], parts[5], parts[6], parts[7], parts[4], grad_out_w,
    )


def solution(mesh):
    acts, row, mat, taps = P("rep", "grp", None), P("grp"), P("grp", None), P(None, "grp")
    in_specs = (acts, row, mat, mat, taps, row, row, row, row, row, mat, acts)
    out_specs = (acts, acts, row, mat, mat, taps, row, row, row, row, row, mat)
    return jax.shard_map(
        per_device, mesh=mesh, in_specs=in_specs, out_specs=out_specs, check_vma=False
    )
```

```python
import jax
import jax.numpy as jnp
from jax import lax
from jax.experimental import pallas as pl
from jax.experimental.pallas import tpu as pltpu
from jax.sharding import PartitionSpec as P

E = 1536
H = 24
P_SIZE = 64
N = 128
K = 4
BLOCK = 256
CH = E + 2 * N
PAD = 128
EPS = 1e-05
FAR = -1e30
SEND = jnp.bfloat16
VMEM = 56 * 1024 * 1024

f32 = jnp.float32
bf16 = jnp.bfloat16


def nn(a, b):
    return lax.dot_general(a, b, (((1,), (0,)), ((), ())), preferred_element_type=f32)


def nt(a, b):
    return lax.dot_general(a, b, (((1,), (1,)), ((), ())), preferred_element_type=f32)


def tn(a, b):
    return lax.dot_general(a, b, (((0,), (0,)), ((), ())), preferred_element_type=f32)


def split2(v):
    hi = v.astype(bf16)
    return hi, (v - hi.astype(f32)).astype(bf16)


def split3(v):
    hi = v.astype(bf16)
    rest = v - hi.astype(f32)
    mid = rest.astype(bf16)
    return hi, mid, (rest - mid.astype(f32)).astype(bf16)


def triangle(lower):
    row = lax.broadcasted_iota(jnp.int32, (BLOCK, BLOCK), 0)
    col = lax.broadcasted_iota(jnp.int32, (BLOCK, BLOCK), 1)
    return row >= col if lower else col >= row


def running_sum(mask, v):
    ones = jnp.where(mask, 1.0, 0.0).astype(bf16)
    hi, mid, lo = split3(v)
    return nn(ones, hi) + nn(ones, mid) + nn(ones, lo)


def spread_heads(v, heads2):
    return nn(jnp.concatenate(split2(v), axis=1), heads2)


def sum_heads(v, heads):
    hi, lo = split2(v)
    return nt(hi, heads) + nt(lo, heads)


def softplus(v):
    return jnp.maximum(v, 0.0) + jnp.log1p(jnp.exp(-jnp.abs(v)))


def sigmoid(v):
    return 1.0 / (1.0 + jnp.exp(-v))


def rates(dt, bias, log_rate):
    step = softplus(dt + bias)
    rate = -step * jnp.exp(log_rate)
    cum = running_sum(triangle(True), rate)
    return step, rate, cum


def conv_sum(ext, conv_w, conv_b):
    summed = conv_b
    for k in range(K):
        summed = summed + conv_w[k : k + 1, :] * ext[5 + k : 5 + k + BLOCK, :]
    return summed


def forward_kernel(
    in_ref, cot_ref, pre_ref, w_in_ref, w_dt_ref, cw_ref, cb_ref, bias_ref, log_ref, skip_ref,
    gain_ref, w_out_ref, heads2_ref,
    hid_o, xbc_o, dt_o, norm_o, dgate_o, dy_o, r1_o, start_o, gain_o, skip_o,
    ext, state, inner,
):
    first = pl.program_id(0) == 0

    @pl.when(first)
    def _():
        ext[0:8, :] = jnp.zeros((8, CH), f32)
        state[...] = jnp.zeros_like(state)
        gain_o[...] = jnp.zeros_like(gain_o)
        skip_o[...] = jnp.zeros_like(skip_o)

    values = in_ref[...].astype(f32)
    scale = lax.rsqrt(jnp.mean(values * values, axis=-1, keepdims=True) + EPS)
    hidden = (values * scale * pre_ref[...]).astype(bf16)
    hid_o[...] = hidden
    xbc = nn(hidden, w_in_ref[:, E:])
    xbc_o[...] = xbc
    ext[8:, :] = xbc
    dt = nn(hidden, w_dt_ref[...])
    dt_o[...] = dt
    step, rate, cum = rates(dt, bias_ref[...], log_ref[...])
    last = cum[BLOCK - 1 : BLOCK, :]
    cum_t = cum.T
    summed = conv_sum(ext, cw_ref[...], cb_ref[...])
    tail = ext[BLOCK : BLOCK + 8, :]
    ext[0:8, :] = tail
    mixed = summed * sigmoid(summed)
    x = mixed[:, :E]
    b = mixed[:, E : E + N].astype(bf16)
    c = mixed[:, E + N :].astype(bf16)
    heads2 = heads2_ref[...]
    xd = (x * spread_heads(step, heads2)).astype(bf16)
    scores = nt(c, b)
    mask = triangle(True)
    low_lane = lax.broadcasted_iota(jnp.int32, (BLOCK, PAD), 1) < P_SIZE
    for pair in range(H // 2):
        lanes = slice(pair * PAD, (pair + 1) * PAD)
        part = xd[:, lanes]
        total = None
        for side in range(2):
            h = 2 * pair + side
            far = jnp.where(mask, cum[:, h : h + 1] - cum_t[h : h + 1, :], FAR)
            mixing = (scores * jnp.exp(far)).astype(bf16)
            keep = low_lane if side == 0 else jnp.logical_not(low_lane)
            one = nn(mixing, jnp.where(keep, part, jnp.zeros_like(part)))
            total = one if total is None else total + one
        inner[:, lanes] = total
    start = state[...].astype(bf16)
    start_o[0] = start
    y_inner = inner[...] + nn(c, start) * spread_heads(jnp.exp(cum), heads2)
    to_last = (xd.astype(f32) * spread_heads(jnp.exp(last - cum), heads2)).astype(bf16)
    whole = spread_heads(jnp.broadcast_to(jnp.exp(last), (8, PAD)), heads2)[0:1, :]
    state[...] = whole * state[...] + tn(b, to_last)

    y = y_inner + skip_ref[...] * x
    gate = nn(hidden, w_in_ref[:, :E])
    sig = sigmoid(gate)
    opened = gate * sig
    gated = y * opened
    out_scale = lax.rsqrt(jnp.mean(gated * gated, axis=-1, keepdims=True) + EPS)
    unit = gated * out_scale
    gain = gain_ref[...]
    norm_o[...] = (unit * gain).astype(bf16)
    d_normed = nt(cot_ref[...], w_out_ref[...])
    gain_o[...] += jnp.sum(d_normed * unit, axis=0, keepdims=True)
    d_unit = d_normed * gain
    d_gated = out_scale * (d_unit - unit * jnp.mean(d_unit * unit, axis=-1, keepdims=True))
    dy = d_gated * opened
    dgate_o[...] = (d_gated * y * (sig + opened * (1.0 - sig))).astype(bf16)
    dy_low = dy.astype(bf16)
    dy_o[...] = dy_low
    r1_o[...] = sum_heads(dy_low.astype(f32) * y_inner, heads2[:PAD, :])
    skip_o[...] += jnp.sum(dy * x, axis=0, keepdims=True)


def backward_kernel(
    xbc_ref, before_ref, dt_ref, dy_ref, r1_ref, start_ref, cw_ref, cb_ref, bias_ref, log_ref,
    skip_ref, heads2_ref,
    dxbc_o, ddt_o, gcw_o, gcb_o, gbias_o, glog_o,
    ext, ext_back, d_state, d_inner, d_scores,
):
    step_id = pl.program_id(0)
    steps = pl.num_programs(0)

    @pl.when(step_id == 0)
    def _():
        ext_back[BLOCK:, :] = jnp.zeros((8, CH), f32)
        d_state[...] = jnp.zeros_like(d_state)
        gcw_o[...] = jnp.zeros_like(gcw_o)
        gcb_o[...] = jnp.zeros_like(gcb_o)
        gbias_o[...] = jnp.zeros_like(gbias_o)
        glog_o[...] = jnp.zeros_like(glog_o)

    xbc = xbc_ref[...]
    ext[0:8, :] = jnp.where(step_id == steps - 1, 0.0, before_ref[...])
    ext[8:, :] = xbc
    cw = cw_ref[...]
    summed = conv_sum(ext, cw, cb_ref[...])
    sig = sigmoid(summed)
    mixed = summed * sig
    d_silu = sig + mixed * (1.0 - sig)
    x = mixed[:, :E]
    b = mixed[:, E : E + N].astype(bf16)
    c = mixed[:, E + N :].astype(bf16)
    dt = dt_ref[...]
    step, rate, cum = rates(dt, bias_ref[...], log_ref[...])
    last = cum[BLOCK - 1 : BLOCK, :]
    cum_t = cum.T
    heads2 = heads2_ref[...]
    heads = heads2[:PAD, :]
    step_e = spread_heads(step, heads2)
    xd = (x * step_e).astype(bf16)
    dy = dy_ref[...]
    scores_t = nt(b, c)
    mask = triangle(False)
    low_lane = lax.broadcasted_iota(jnp.int32, (BLOCK, PAD), 1) < P_SIZE
    d_scores[...] = jnp.zeros_like(d_scores)
    for pair in range(H // 2):
        lanes = slice(pair * PAD, (pair + 1) * PAD)
        part = xd[:, lanes]
        dpart = dy[:, lanes]
        total = None
        for side in range(2):
            h = 2 * pair + side
            far = jnp.where(mask, cum_t[h : h + 1, :] - cum[:, h : h + 1], FAR)
            decay = jnp.exp(far)
            mixing = (scores_t * decay).astype(bf16)
            keep = low_lane if side == 0 else jnp.logical_not(low_lane)
            d_scores[...] += nt(jnp.where(keep, part, jnp.zeros_like(part)), dpart) * decay
            one = nn(mixing, jnp.where(keep, dpart, jnp.zeros_like(dpart)))
            total = one if total is None else total + one
        d_inner[:, lanes] = total
    start = start_ref[0]
    d_last = d_state[...]
    d_last_low = d_last.astype(bf16)
    to_last = spread_heads(jnp.exp(last - cum), heads2)
    carried = to_last * nn(b, d_last_low)
    dxd = d_inner[...] + carried
    xd32 = xd.astype(f32)
    whole = spread_heads(jnp.broadcast_to(jnp.exp(last), (8, PAD)), heads2)[0:1, :]
    end_row = jnp.sum(xd32 * carried, axis=0, keepdims=True) + whole * jnp.sum(
        d_last * start.astype(f32), axis=0, keepdims=True
    )
    r3 = sum_heads(jnp.broadcast_to(end_row, (8, E)), heads)[0:1, :]
    row = lax.broadcasted_iota(jnp.int32, (BLOCK, PAD), 0)
    d_cum = r1_ref[...] - sum_heads(xd32 * dxd, heads) + jnp.where(row == BLOCK - 1, r3, 0.0)
    d_rate = running_sum(triangle(False), d_cum)
    d_step = sum_heads(dxd * x, heads) - jnp.exp(log_ref[...]) * d_rate
    glog_o[...] += jnp.sum(d_rate * rate, axis=0, keepdims=True)
    ddt = d_step * sigmoid(dt + bias_ref[...])
    gbias_o[...] += jnp.sum(ddt, axis=0, keepdims=True)
    ddt_o[...] = ddt.astype(bf16)
    dy32 = dy.astype(f32)
    dx = dxd * step_e + skip_ref[...] * dy32
    dy_e = (dy32 * spread_heads(jnp.exp(cum), heads2)).astype(bf16)
    weighted = (xd32 * to_last).astype(bf16)
    d_sc = d_scores[...].astype(bf16)
    d_c = tn(d_sc, b) + nt(dy_e, start)
    d_b = nn(d_sc, c) + nt(weighted, d_last_low)
    d_state[...] = whole * d_last + tn(c, dy_e)
    d_sum = jnp.concatenate([dx, d_b, d_c], axis=1) * d_silu
    gcb_o[...] += jnp.sum(d_sum, axis=0, keepdims=True)
    ext_back[0:BLOCK, :] = d_sum
    total = None
    for k in range(K):
        later = ext_back[K - 1 - k : K - 1 - k + BLOCK, :]
        gcw_o[k : k + 1, :] += jnp.sum(xbc * later, axis=0, keepdims=True)
        one = cw[k : k + 1, :] * later
        total = one if total is None else total + one
    dxbc_o[...] = total.astype(bf16)
    head = ext_back[0:8, :]
    ext_back[BLOCK:, :] = head


def whole_spec(shape):
    return pl.BlockSpec(shape, lambda i: tuple(0 for _ in shape))


def forward_call(seq, cot, pre, w_in, w_dt, cw, cb, bias, log_rate, skip, gain, w_out, heads2):
    tokens, width = seq.shape
    blocks = tokens // BLOCK
    rows = lambda n: pl.BlockSpec((BLOCK, n), lambda i: (i, 0))
    out = jax.ShapeDtypeStruct
    weights = (pre, w_in, w_dt, cw, cb, bias, log_rate, skip, gain, w_out, heads2)
    return pl.pallas_call(
        forward_kernel,
        grid=(blocks,),
        in_specs=[rows(width), rows(width)] + [whole_spec(w.shape) for w in weights],
        out_specs=[
            rows(width), rows(CH), rows(PAD), rows(E), rows(E), rows(E), rows(PAD),
            pl.BlockSpec((1, N, E), lambda i: (i, 0, 0)),
            whole_spec((1, E)), whole_spec((1, E)),
        ],
        out_shape=[
            out((tokens, width), bf16), out((tokens, CH), f32), out((tokens, PAD), f32),
            out((tokens, E), bf16), out((tokens, E), bf16), out((tokens, E), bf16),
            out((tokens, PAD), f32), out((blocks, N, E), bf16), out((1, E), f32), out((1, E), f32),
        ],
        scratch_shapes=[
            pltpu.VMEM((BLOCK + 8, CH), f32), pltpu.VMEM((N, E), f32), pltpu.VMEM((BLOCK, E), f32),
        ],
        compiler_params=pltpu.CompilerParams(vmem_limit_bytes=VMEM),
        cost_estimate=pl.CostEstimate(
            flops=20_000_000_000, bytes_accessed=40_000_000, transcendentals=12_000_000
        ),
        name="mixer_forward",
    )(seq, cot, *weights)


def backward_call(xbc, dt, dy, r1, starts, cw, cb, bias, log_rate, skip, heads2):
    tokens = xbc.shape[0]
    blocks = tokens // BLOCK
    per = BLOCK // 8
    rows = lambda n: pl.BlockSpec((BLOCK, n), lambda i: (blocks - 1 - i, 0))
    out = jax.ShapeDtypeStruct
    weights = (cw, cb, bias, log_rate, skip, heads2)
    return pl.pallas_call(
        backward_kernel,
        grid=(blocks,),
        in_specs=[
            rows(CH),
            pl.BlockSpec((8, CH), lambda i: (jnp.maximum((blocks - 1 - i) * per - 1, 0), 0)),
            rows(PAD), rows(E), rows(PAD),
            pl.BlockSpec((1, N, E), lambda i: (blocks - 1 - i, 0, 0)),
        ]
        + [whole_spec(w.shape) for w in weights],
        out_specs=[
            rows(CH), rows(PAD), whole_spec((K, CH)), whole_spec((1, CH)), whole_spec((1, PAD)),
            whole_spec((1, PAD)),
        ],
        out_shape=[
            out((tokens, CH), bf16), out((tokens, PAD), bf16), out((K, CH), f32),
            out((1, CH), f32), out((1, PAD), f32), out((1, PAD), f32),
        ],
        scratch_shapes=[
            pltpu.VMEM((BLOCK + 8, CH), f32), pltpu.VMEM((BLOCK + 8, CH), f32),
            pltpu.VMEM((N, E), f32), pltpu.VMEM((BLOCK, E), f32), pltpu.VMEM((BLOCK, BLOCK), f32),
        ],
        compiler_params=pltpu.CompilerParams(vmem_limit_bytes=VMEM),
        cost_estimate=pl.CostEstimate(
            flops=20_000_000_000, bytes_accessed=30_000_000, transcendentals=12_000_000
        ),
        name="mixer_backward",
    )(xbc, xbc, dt, dy, r1, starts, *weights)


SWAP = [(0, 1), (1, 0)]


def to_sequence(pieces, mine):
    kept = lax.dynamic_index_in_dim(pieces, mine, 0, keepdims=False)
    other = lax.ppermute(lax.dynamic_index_in_dim(pieces, 1 - mine, 0, keepdims=False), "grp", SWAP)
    early = jnp.where(mine == 0, kept, other)
    late = jnp.where(mine == 0, other, kept)
    return jnp.concatenate([early, late], axis=0)


def to_pieces(seq, mine):
    halves = seq.reshape(2, seq.shape[0] // 2, seq.shape[1])
    kept = lax.dynamic_index_in_dim(halves, mine, 0, keepdims=False)
    other = lax.ppermute(lax.dynamic_index_in_dim(halves, 1 - mine, 0, keepdims=False), "grp", SWAP)
    return jnp.where(mine == 0, jnp.stack([kept, other]), jnp.stack([other, kept]))


def pad_heads(v):
    return jnp.pad(v, [(0, 0)] * (v.ndim - 1) + [(0, PAD - H)])


def flipped(v, bit):
    size = lax.axis_size("rep")
    return lax.ppermute(v, "rep", [(i, i ^ (1 << bit)) for i in range(size)])


def bit_of(bit):
    return (lax.axis_index("rep") >> bit) & 1


def in_order(kept, other, high, axis=0):
    first = jnp.where(high == 0, kept, other)
    second = jnp.where(high == 0, other, kept)
    return jnp.concatenate([first, second], axis=axis)


def gathered_rows(shard, mine):
    rows, columns = shard.shape
    quarter = rows // 4
    place = lax.axis_index("rep") & 3
    part = lax.dynamic_slice_in_dim(shard, place * quarter, quarter, axis=0)
    part = lax.ppermute(part, "grp", SWAP)[None, None]
    part = in_order(part, flipped(part, 1), bit_of(1), axis=0)
    part = in_order(part, flipped(part, 0), bit_of(0), axis=1)
    return in_order(shard, part.reshape(rows, columns), mine)


def summed_over_all(halves, mine):
    kept = lax.dynamic_index_in_dim(halves, mine, 0, keepdims=False)
    sent = lax.dynamic_index_in_dim(halves, 1 - mine, 0, keepdims=False).astype(SEND)
    total = kept + lax.ppermute(sent, "grp", SWAP).astype(f32)
    bits = (lax.axis_size("rep") - 1).bit_length()
    for bit in range(bits):
        half = total.shape[0] // 2
        high = bit_of(bit)
        kept = lax.dynamic_slice_in_dim(total, high * half, half, axis=0)
        sent = lax.dynamic_slice_in_dim(total, (1 - high) * half, half, axis=0).astype(SEND)
        total = kept + flipped(sent, bit).astype(f32)
    total = total.astype(SEND)
    for bit in reversed(range(bits)):
        total = in_order(total, flipped(total, bit), bit_of(bit))
    return total.astype(f32)


def summed_small(halves, mine):
    kept = lax.dynamic_index_in_dim(halves, mine, 0, keepdims=False)
    sent = lax.dynamic_index_in_dim(halves, 1 - mine, 0, keepdims=False)
    total = kept + lax.ppermute(sent, "grp", SWAP)
    for bit in range((lax.axis_size("rep") - 1).bit_length()):
        total = total + flipped(total, bit)
    return total


def per_device(
    inputs, pre_gain, w_in, w_dt, conv_w, conv_b, dt_bias, a_log, d_skip, norm_gain, w_out,
    cotangent,
):
    mine = lax.axis_index("grp")
    vectors = jnp.concatenate(
        [conv_w.reshape(-1), pre_gain, conv_b, dt_bias, a_log, d_skip, norm_gain, w_dt.reshape(-1)]
    )
    both = in_order(vectors[None], lax.ppermute(vectors[None], "grp", SWAP), mine)
    sizes = [conv_w.size, pre_gain.size, conv_b.size, H // 2, H // 2, H // 2, norm_gain.size]
    cuts, at = [], 0
    for size in sizes:
        cuts.append(both[:, at : at + size])
        at += size
    half = conv_w.shape[1]
    cw = cuts[0].reshape(2, K, half).transpose(1, 0, 2).reshape(K, CH).astype(f32)
    pre, cb, bias, log_rate, skip, gain = (v.reshape(1, -1).astype(f32) for v in cuts[1:])
    wdt = pad_heads(both[:, at:].reshape(-1, H))
    bias, log_rate = pad_heads(bias), pad_heads(log_rate)
    skip = jnp.repeat(skip, P_SIZE, axis=1)
    win = gathered_rows(w_in, mine)
    wout = gathered_rows(w_out, mine)
    heads = (jnp.arange(PAD)[:, None] == jnp.arange(E)[None, :] // P_SIZE).astype(bf16)
    heads2 = jnp.concatenate([heads, heads], axis=0)
    seq = to_sequence(inputs, mine)
    cot = to_sequence(cotangent, mine)
    hidden, xbc, dt, normed, d_gate, dy, r1, starts, g_gain, g_skip = forward_call(
        seq, cot, pre, win, wdt, cw, cb, bias, log_rate, skip, gain, wout, heads2
    )
    g_out = tn(normed, cot).reshape(2, E // 2, -1)
    g_gate = tn(hidden, d_gate).reshape(2, -1, E)
    early = jnp.concatenate([g_out, g_gate[:, :, : E // 2], g_gate[:, :, E // 2 :]], axis=1)
    early = summed_over_all(early, mine)
    third = w_in.shape[0]
    grad_out_w = early[: E // 2]
    grad_gate_w = jnp.concatenate([early[E // 2 : E // 2 + third], early[E // 2 + third :]], axis=1)
    result = to_pieces((seq.astype(f32) + nn(normed, wout)).astype(bf16), mine)
    d_xbc, d_dt, g_cw, g_cb, g_bias, g_log = backward_call(
        xbc, dt, dy, r1, starts, cw, cb, bias, log_rate, skip, heads2
    )
    grad_xbc_w = summed_over_all(tn(hidden, d_xbc).reshape(2, -1, CH), mine)
    grad_in_w = jnp.concatenate([grad_gate_w, grad_xbc_w], axis=1)
    d_hidden = nt(d_gate, win[:, :E]) + nt(d_xbc, win[:, E:]) + nt(d_dt, wdt)
    seq32 = seq.astype(f32)
    scale = lax.rsqrt(jnp.mean(seq32 * seq32, axis=-1, keepdims=True) + EPS)
    unit = seq32 * scale
    g_pre = jnp.sum(d_hidden * unit, axis=0)
    d_unit = d_hidden * pre
    d_seq = scale * (d_unit - unit * jnp.mean(d_unit * unit, axis=-1, keepdims=True))
    d_inputs = to_pieces((cot.astype(f32) + d_seq).astype(bf16), mine)
    g_wdt = tn(hidden, d_dt)[:, :H]
    g_skip_h = g_skip.reshape(H, P_SIZE).sum(axis=1)
    small = jnp.concatenate(
        [
            g_wdt.reshape(2, -1), g_pre.reshape(2, -1),
            g_cw.reshape(K, 2, half).transpose(1, 0, 2).reshape(2, -1), g_cb.reshape(2, -1),
            g_gain.reshape(2, -1), g_bias[0, :H].reshape(2, -1), g_log[0, :H].reshape(2, -1),
            g_skip_h.reshape(2, -1),
        ],
        axis=1,
    )
    small = summed_small(small, mine)
    parts, at = [], 0
    for size in (w_dt.size, pre_gain.size, conv_w.size, half, norm_gain.size, 12, 12, 12):
        parts.append(small[at : at + size])
        at += size
    return (
        result, d_inputs, parts[1], grad_in_w, parts[0].reshape(w_dt.shape),
        parts[2].reshape(K, half), parts[3], parts[5], parts[6], parts[7], parts[4], grad_out_w,
    )


def solution(mesh):
    acts, row, mat, taps = P("rep", "grp", None), P("grp"), P("grp", None), P(None, "grp")
    in_specs = (acts, row, mat, mat, taps, row, row, row, row, row, mat, acts)
    out_specs = (acts, acts, row, mat, mat, taps, row, row, row, row, row, mat)
    return jax.shard_map(
        per_device, mesh=mesh, in_specs=in_specs, out_specs=out_specs, check_vma=False
    )
```

```python
import functools

import jax
import jax.numpy as jnp
from jax import lax
from jax.experimental import pallas as pl
from jax.experimental.pallas import tpu as pltpu
from jax.sharding import PartitionSpec as P

E = 1536
H = 24
P_SIZE = 64
N = 128
K = 4
BLOCK = 256
CH = E + 2 * N
PAD = 128
EPS = 1e-05
FAR = -1e30
SEND = jnp.bfloat16
VMEM = 56 * 1024 * 1024

f32 = jnp.float32
bf16 = jnp.bfloat16


def nn(a, b):
    return lax.dot_general(a, b, (((1,), (0,)), ((), ())), preferred_element_type=f32)


def nt(a, b):
    return lax.dot_general(a, b, (((1,), (1,)), ((), ())), preferred_element_type=f32)


def tn(a, b):
    return lax.dot_general(a, b, (((0,), (0,)), ((), ())), preferred_element_type=f32)


def split2(v):
    hi = v.astype(bf16)
    return hi, (v - hi.astype(f32)).astype(bf16)


def split3(v):
    hi = v.astype(bf16)
    rest = v - hi.astype(f32)
    mid = rest.astype(bf16)
    return hi, mid, (rest - mid.astype(f32)).astype(bf16)


def triangle(lower):
    row = lax.broadcasted_iota(jnp.int32, (BLOCK, BLOCK), 0)
    col = lax.broadcasted_iota(jnp.int32, (BLOCK, BLOCK), 1)
    return row >= col if lower else col >= row


def running_sum(mask, v):
    ones = jnp.where(mask, 1.0, 0.0).astype(bf16)
    hi, mid, lo = split3(v)
    return nn(ones, hi) + nn(ones, mid) + nn(ones, lo)


def spread_heads(v, heads2):
    return nn(jnp.concatenate(split2(v), axis=1), heads2)


def sum_heads(v, heads):
    hi, lo = split2(v)
    return nt(hi, heads) + nt(lo, heads)


def softplus(v):
    return jnp.maximum(v, 0.0) + jnp.log1p(jnp.exp(-jnp.abs(v)))


def sigmoid(v):
    return 1.0 / (1.0 + jnp.exp(-v))


def rates(dt, bias, log_rate):
    step = softplus(dt + bias)
    rate = -step * jnp.exp(log_rate)
    cum = running_sum(triangle(True), rate)
    return step, rate, cum


def conv_sum(ext, conv_w, conv_b):
    summed = conv_b
    for k in range(K):
        summed = summed + conv_w[k : k + 1, :] * ext[5 + k : 5 + k + BLOCK, :]
    return summed


def forward_kernel(
    in_ref, pre_ref, w_xbc_ref, w_dt_ref, cw_ref, cb_ref, bias_ref, log_ref, heads2_ref,
    hid_o, xbc_o, dt_o, x_o, y_o, start_o,
    ext, state, inner,
):
    first = pl.program_id(0) == 0

    @pl.when(first)
    def _():
        ext[0:8, :] = jnp.zeros((8, CH), f32)
        state[...] = jnp.zeros_like(state)

    values = in_ref[...].astype(f32)
    scale = lax.rsqrt(jnp.mean(values * values, axis=-1, keepdims=True) + EPS)
    hidden = (values * scale * pre_ref[...]).astype(bf16)
    hid_o[...] = hidden
    xbc = nn(hidden, w_xbc_ref[...])
    xbc_o[...] = xbc
    ext[8:, :] = xbc
    dt = nn(hidden, w_dt_ref[...])
    dt_o[...] = dt
    step, rate, cum = rates(dt, bias_ref[...], log_ref[...])
    last = cum[BLOCK - 1 : BLOCK, :]
    cum_t = cum.T
    summed = conv_sum(ext, cw_ref[...], cb_ref[...])
    tail = ext[BLOCK : BLOCK + 8, :]
    ext[0:8, :] = tail
    mixed = summed * sigmoid(summed)
    x = mixed[:, :E]
    b = mixed[:, E : E + N].astype(bf16)
    c = mixed[:, E + N :].astype(bf16)
    heads2 = heads2_ref[...]
    xd = (x * spread_heads(step, heads2)).astype(bf16)
    scores = nt(c, b)
    mask = triangle(True)
    low_lane = lax.broadcasted_iota(jnp.int32, (BLOCK, PAD), 1) < P_SIZE
    for pair in range(H // 2):
        lanes = slice(pair * PAD, (pair + 1) * PAD)
        part = xd[:, lanes]
        total = None
        for side in range(2):
            h = 2 * pair + side
            far = jnp.where(mask, cum[:, h : h + 1] - cum_t[h : h + 1, :], FAR)
            mixing = (scores * jnp.exp(far)).astype(bf16)
            keep = low_lane if side == 0 else jnp.logical_not(low_lane)
            one = nn(mixing, jnp.where(keep, part, jnp.zeros_like(part)))
            total = one if total is None else total + one
        inner[:, lanes] = total
    start = state[...].astype(bf16)
    start_o[0] = start
    y_o[...] = inner[...] + nn(c, start) * spread_heads(jnp.exp(cum), heads2)
    x_o[...] = x
    to_last = (xd.astype(f32) * spread_heads(jnp.exp(last - cum), heads2)).astype(bf16)
    whole = spread_heads(jnp.broadcast_to(jnp.exp(last), (8, PAD)), heads2)[0:1, :]
    state[...] = whole * state[...] + tn(b, to_last)


def gate_kernel(
    hid_ref, x_ref, y_ref, cot_ref, w_gate_ref, skip_ref, gain_ref, w_out_ref, heads2_ref,
    norm_o, dgate_o, dy_o, r1_o, gain_o, skip_o,
):
    @pl.when(pl.program_id(0) == 0)
    def _():
        gain_o[...] = jnp.zeros_like(gain_o)
        skip_o[...] = jnp.zeros_like(skip_o)

    x = x_ref[...]
    y_inner = y_ref[...]
    heads2 = heads2_ref[...]
    y = y_inner + skip_ref[...] * x
    gate = nn(hid_ref[...], w_gate_ref[...])
    sig = sigmoid(gate)
    opened = gate * sig
    gated = y * opened
    out_scale = lax.rsqrt(jnp.mean(gated * gated, axis=-1, keepdims=True) + EPS)
    unit = gated * out_scale
    gain = gain_ref[...]
    norm_o[...] = (unit * gain).astype(bf16)
    d_normed = nt(cot_ref[...], w_out_ref[...])
    gain_o[...] += jnp.sum(d_normed * unit, axis=0, keepdims=True)
    d_unit = d_normed * gain
    d_gated = out_scale * (d_unit - unit * jnp.mean(d_unit * unit, axis=-1, keepdims=True))
    dy = d_gated * opened
    dgate_o[...] = (d_gated * y * (sig + opened * (1.0 - sig))).astype(bf16)
    dy_low = dy.astype(bf16)
    dy_o[...] = dy_low
    r1_o[...] = sum_heads(dy_low.astype(f32) * y_inner, heads2[:PAD, :])
    skip_o[...] += jnp.sum(dy * x, axis=0, keepdims=True)


def backward_kernel(
    end, xbc_ref, before_ref, dt_ref, dy_ref, r1_ref, start_ref, cw_ref, cb_ref, bias_ref, log_ref,
    skip_ref, heads2_ref, state_ref, head_ref,
    dxbc_o, ddt_o, gcw_o, gcb_o, gbias_o, glog_o, state_o, head_o,
    ext, ext_back, d_state, d_inner, d_scores,
):
    step_id = pl.program_id(0)

    @pl.when(step_id == 0)
    def _():
        ext_back[BLOCK:, :] = head_ref[...]
        d_state[...] = state_ref[...]
        gcw_o[...] = jnp.zeros_like(gcw_o)
        gcb_o[...] = jnp.zeros_like(gcb_o)
        gbias_o[...] = jnp.zeros_like(gbias_o)
        glog_o[...] = jnp.zeros_like(glog_o)

    xbc = xbc_ref[...]
    ext[0:8, :] = jnp.where(step_id == end - 1, 0.0, before_ref[...])
    ext[8:, :] = xbc
    cw = cw_ref[...]
    summed = conv_sum(ext, cw, cb_ref[...])
    sig = sigmoid(summed)
    mixed = summed * sig
    d_silu = sig + mixed * (1.0 - sig)
    x = mixed[:, :E]
    b = mixed[:, E : E + N].astype(bf16)
    c = mixed[:, E + N :].astype(bf16)
    dt = dt_ref[...]
    step, rate, cum = rates(dt, bias_ref[...], log_ref[...])
    last = cum[BLOCK - 1 : BLOCK, :]
    cum_t = cum.T
    heads2 = heads2_ref[...]
    heads = heads2[:PAD, :]
    step_e = spread_heads(step, heads2)
    xd = (x * step_e).astype(bf16)
    dy = dy_ref[...]
    scores_t = nt(b, c)
    mask = triangle(False)
    low_lane = lax.broadcasted_iota(jnp.int32, (BLOCK, PAD), 1) < P_SIZE
    d_scores[...] = jnp.zeros_like(d_scores)
    for pair in range(H // 2):
        lanes = slice(pair * PAD, (pair + 1) * PAD)
        part = xd[:, lanes]
        dpart = dy[:, lanes]
        total = None
        for side in range(2):
            h = 2 * pair + side
            far = jnp.where(mask, cum_t[h : h + 1, :] - cum[:, h : h + 1], FAR)
            decay = jnp.exp(far)
            mixing = (scores_t * decay).astype(bf16)
            keep = low_lane if side == 0 else jnp.logical_not(low_lane)
            d_scores[...] += nt(jnp.where(keep, part, jnp.zeros_like(part)), dpart) * decay
            one = nn(mixing, jnp.where(keep, dpart, jnp.zeros_like(dpart)))
            total = one if total is None else total + one
        d_inner[:, lanes] = total
    start = start_ref[0]
    d_last = d_state[...]
    d_last_low = d_last.astype(bf16)
    to_last = spread_heads(jnp.exp(last - cum), heads2)
    carried = to_last * nn(b, d_last_low)
    dxd = d_inner[...] + carried
    xd32 = xd.astype(f32)
    whole = spread_heads(jnp.broadcast_to(jnp.exp(last), (8, PAD)), heads2)[0:1, :]
    end_row = jnp.sum(xd32 * carried, axis=0, keepdims=True) + whole * jnp.sum(
        d_last * start.astype(f32), axis=0, keepdims=True
    )
    r3 = sum_heads(jnp.broadcast_to(end_row, (8, E)), heads)[0:1, :]
    row = lax.broadcasted_iota(jnp.int32, (BLOCK, PAD), 0)
    d_cum = r1_ref[...] - sum_heads(xd32 * dxd, heads) + jnp.where(row == BLOCK - 1, r3, 0.0)
    d_rate = running_sum(triangle(False), d_cum)
    d_step = sum_heads(dxd * x, heads) - jnp.exp(log_ref[...]) * d_rate
    glog_o[...] += jnp.sum(d_rate * rate, axis=0, keepdims=True)
    ddt = d_step * sigmoid(dt + bias_ref[...])
    gbias_o[...] += jnp.sum(ddt, axis=0, keepdims=True)
    ddt_o[...] = ddt.astype(bf16)
    dy32 = dy.astype(f32)
    dx = dxd * step_e + skip_ref[...] * dy32
    dy_e = (dy32 * spread_heads(jnp.exp(cum), heads2)).astype(bf16)
    weighted = (xd32 * to_last).astype(bf16)
    d_sc = d_scores[...].astype(bf16)
    d_c = tn(d_sc, b) + nt(dy_e, start)
    d_b = nn(d_sc, c) + nt(weighted, d_last_low)
    d_state[...] = whole * d_last + tn(c, dy_e)
    d_sum = jnp.concatenate([dx, d_b, d_c], axis=1) * d_silu
    gcb_o[...] += jnp.sum(d_sum, axis=0, keepdims=True)
    ext_back[0:BLOCK, :] = d_sum
    total = None
    for k in range(K):
        later = ext_back[K - 1 - k : K - 1 - k + BLOCK, :]
        gcw_o[k : k + 1, :] += jnp.sum(xbc * later, axis=0, keepdims=True)
        one = cw[k : k + 1, :] * later
        total = one if total is None else total + one
    dxbc_o[...] = total.astype(bf16)
    head = ext_back[0:8, :]
    ext_back[BLOCK:, :] = head
    head_o[...] = head
    state_o[...] = d_state[...]


def whole_spec(shape):
    return pl.BlockSpec(shape, lambda i: tuple(0 for _ in shape))


def forward_call(seq, pre, w_xbc, w_dt, cw, cb, bias, log_rate, heads2):
    tokens, width = seq.shape
    blocks = tokens // BLOCK
    rows = lambda n: pl.BlockSpec((BLOCK, n), lambda i: (i, 0))
    out = jax.ShapeDtypeStruct
    weights = (pre, w_xbc, w_dt, cw, cb, bias, log_rate, heads2)
    return pl.pallas_call(
        forward_kernel,
        grid=(blocks,),
        in_specs=[rows(width)] + [whole_spec(w.shape) for w in weights],
        out_specs=[
            rows(width), rows(CH), rows(PAD), rows(E), rows(E),
            pl.BlockSpec((1, N, E), lambda i: (i, 0, 0)),
        ],
        out_shape=[
            out((tokens, width), bf16), out((tokens, CH), f32), out((tokens, PAD), f32),
            out((tokens, E), f32), out((tokens, E), f32), out((blocks, N, E), bf16),
        ],
        scratch_shapes=[
            pltpu.VMEM((BLOCK + 8, CH), f32), pltpu.VMEM((N, E), f32), pltpu.VMEM((BLOCK, E), f32),
        ],
        compiler_params=pltpu.CompilerParams(vmem_limit_bytes=VMEM),
        cost_estimate=pl.CostEstimate(
            flops=20_000_000_000, bytes_accessed=40_000_000, transcendentals=12_000_000
        ),
        name="mixer_forward",
    )(seq, *weights)


def gate_call(hidden, x, y, cot, w_gate, skip, gain, w_out, heads2):
    tokens, width = hidden.shape
    rows = lambda n: pl.BlockSpec((BLOCK, n), lambda i: (i, 0))
    out = jax.ShapeDtypeStruct
    weights = (w_gate, skip, gain, w_out, heads2)
    return pl.pallas_call(
        gate_kernel,
        grid=(tokens // BLOCK,),
        in_specs=[rows(width), rows(E), rows(E), rows(width)]
        + [whole_spec(w.shape) for w in weights],
        out_specs=[
            rows(E), rows(E), rows(E), rows(PAD), whole_spec((1, E)), whole_spec((1, E)),
        ],
        out_shape=[
            out((tokens, E), bf16), out((tokens, E), bf16), out((tokens, E), bf16),
            out((tokens, PAD), f32), out((1, E), f32), out((1, E), f32),
        ],
        compiler_params=pltpu.CompilerParams(vmem_limit_bytes=VMEM),
        cost_estimate=pl.CostEstimate(
            flops=6_000_000_000, bytes_accessed=30_000_000, transcendentals=3_000_000
        ),
        name="gated_norm",
    )(hidden, x, y, cot, *weights)


def backward_call(begin, end, xbc, dt, dy, r1, starts, weights, d_state, head):
    per = BLOCK // 8
    tokens = (end - begin) * BLOCK
    rows = lambda n: pl.BlockSpec((BLOCK, n), lambda i: (end - 1 - i, 0))
    outs = lambda n: pl.BlockSpec((BLOCK, n), lambda i: (end - begin - 1 - i, 0))
    out = jax.ShapeDtypeStruct
    weights = (*weights, d_state, head)
    return pl.pallas_call(
        functools.partial(backward_kernel, end),
        grid=(end - begin,),
        in_specs=[
            rows(CH),
            pl.BlockSpec((8, CH), lambda i: (jnp.maximum((end - 1 - i) * per - 1, 0), 0)),
            rows(PAD), rows(E), rows(PAD),
            pl.BlockSpec((1, N, E), lambda i: (end - 1 - i, 0, 0)),
        ]
        + [whole_spec(w.shape) for w in weights],
        out_specs=[
            outs(CH), outs(PAD), whole_spec((K, CH)), whole_spec((1, CH)), whole_spec((1, PAD)),
            whole_spec((1, PAD)), whole_spec((N, E)), whole_spec((8, CH)),
        ],
        out_shape=[
            out((tokens, CH), bf16), out((tokens, PAD), bf16), out((K, CH), f32),
            out((1, CH), f32), out((1, PAD), f32), out((1, PAD), f32), out((N, E), f32),
            out((8, CH), f32),
        ],
        scratch_shapes=[
            pltpu.VMEM((BLOCK + 8, CH), f32), pltpu.VMEM((BLOCK + 8, CH), f32),
            pltpu.VMEM((N, E), f32), pltpu.VMEM((BLOCK, E), f32), pltpu.VMEM((BLOCK, BLOCK), f32),
        ],
        compiler_params=pltpu.CompilerParams(vmem_limit_bytes=VMEM),
        cost_estimate=pl.CostEstimate(
            flops=20_000_000_000, bytes_accessed=20_000_000, transcendentals=6_000_000
        ),
        name="mixer_backward",
    )(xbc, xbc, dt, dy, r1, starts, *weights)


SWAP = [(0, 1), (1, 0)]


def to_sequence(pieces, mine):
    kept = lax.dynamic_index_in_dim(pieces, mine, 0, keepdims=False)
    other = lax.ppermute(lax.dynamic_index_in_dim(pieces, 1 - mine, 0, keepdims=False), "grp", SWAP)
    early = jnp.where(mine == 0, kept, other)
    late = jnp.where(mine == 0, other, kept)
    return jnp.concatenate([early, late], axis=0)


def to_pieces(seq, mine):
    halves = seq.reshape(2, seq.shape[0] // 2, seq.shape[1])
    kept = lax.dynamic_index_in_dim(halves, mine, 0, keepdims=False)
    other = lax.ppermute(lax.dynamic_index_in_dim(halves, 1 - mine, 0, keepdims=False), "grp", SWAP)
    return jnp.where(mine == 0, jnp.stack([kept, other]), jnp.stack([other, kept]))


def pad_heads(v):
    return jnp.pad(v, [(0, 0)] * (v.ndim - 1) + [(0, PAD - H)])


def flipped(v, bit):
    size = lax.axis_size("rep")
    return lax.ppermute(v, "rep", [(i, i ^ (1 << bit)) for i in range(size)])


def bit_of(bit):
    return (lax.axis_index("rep") >> bit) & 1


def in_order(kept, other, high, axis=0):
    first = jnp.where(high == 0, kept, other)
    second = jnp.where(high == 0, other, kept)
    return jnp.concatenate([first, second], axis=axis)


def gathered_rows(shard, mine):
    rows, columns = shard.shape
    quarter = rows // 4
    place = lax.axis_index("rep") & 3
    part = lax.dynamic_slice_in_dim(shard, place * quarter, quarter, axis=0)
    part = lax.ppermute(part, "grp", SWAP)[None, None]
    part = in_order(part, flipped(part, 1), bit_of(1), axis=0)
    part = in_order(part, flipped(part, 0), bit_of(0), axis=1)
    return in_order(shard, part.reshape(rows, columns), mine)


def halved(halves, mine):
    kept = lax.dynamic_index_in_dim(halves, mine, 0, keepdims=False)
    sent = lax.dynamic_index_in_dim(halves, 1 - mine, 0, keepdims=False)
    return kept, sent.astype(SEND)


def core_halves(v):
    half = v.shape[1] // 2
    high = bit_of(0)
    kept = lax.dynamic_slice_in_dim(v, high * half, half, axis=1)
    sent = lax.dynamic_slice_in_dim(v, (1 - high) * half, half, axis=1)
    return kept, sent.astype(SEND)


def shifted(v, bit, count, mask):
    size = lax.axis_size("rep")
    return lax.ppermute(v, "rep", [(i, i ^ (mask << bit)) for i in range(size)])


def summed_over_rest(total):
    bits = (lax.axis_size("rep") - 1).bit_length()
    groups = [(1, 1)] + [(b, min(2, bits - b)) for b in range(2, bits, 2)]
    for bit, width in groups:
        count = 1 << width
        me = (lax.axis_index("rep") >> bit) & (count - 1)
        size = total.shape[0] // count
        part = lambda mask: lax.dynamic_slice_in_dim(total, (me ^ mask) * size, size, axis=0)
        come = [shifted(part(m).astype(SEND), bit, count, m) for m in range(1, count)]
        total = sum((v.astype(f32) for v in come), part(0))
    total = total.astype(SEND)
    for bit, width in reversed(groups):
        count = 1 << width
        me = (lax.axis_index("rep") >> bit) & (count - 1)
        parts = [total] + [shifted(total, bit, count, m) for m in range(1, count)]
        ordered = []
        for place in range(count):
            pick = parts[0]
            for m in range(1, count):
                pick = jnp.where((me ^ m) == place, parts[m], pick)
            ordered.append(pick)
        total = jnp.concatenate(ordered, axis=0)
    return total


def summed_small(halves, mine):
    kept = lax.dynamic_index_in_dim(halves, mine, 0, keepdims=False)
    sent = lax.dynamic_index_in_dim(halves, 1 - mine, 0, keepdims=False)
    total = kept + lax.ppermute(sent, "grp", SWAP)
    for bit in range((lax.axis_size("rep") - 1).bit_length()):
        total = total + flipped(total, bit)
    return total


def per_device(
    inputs, pre_gain, w_in, w_dt, conv_w, conv_b, dt_bias, a_log, d_skip, norm_gain, w_out,
    cotangent,
):
    mine = lax.axis_index("grp")
    vectors = jnp.concatenate(
        [conv_w.reshape(-1), pre_gain, conv_b, dt_bias, a_log, d_skip, norm_gain, w_dt.reshape(-1)]
    )
    both = in_order(vectors[None], lax.ppermute(vectors[None], "grp", SWAP), mine)
    sizes = [conv_w.size, pre_gain.size, conv_b.size, H // 2, H // 2, H // 2, norm_gain.size]
    cuts, at = [], 0
    for size in sizes:
        cuts.append(both[:, at : at + size])
        at += size
    half = conv_w.shape[1]
    cw = cuts[0].reshape(2, K, half).transpose(1, 0, 2).reshape(K, CH).astype(f32)
    pre, cb, bias, log_rate, skip, gain = (v.reshape(1, -1).astype(f32) for v in cuts[1:])
    wdt = pad_heads(both[:, at:].reshape(-1, H))
    bias, log_rate = pad_heads(bias), pad_heads(log_rate)
    skip = jnp.repeat(skip, P_SIZE, axis=1)
    seq = to_sequence(inputs, mine)
    w_xbc = gathered_rows(w_in[:, E:], mine)
    w_gate, w_out, cotangent, _, _ = lax.optimization_barrier(
        (w_in[:, :E], w_out, cotangent, seq, w_xbc)
    )
    w_gate = gathered_rows(w_gate, mine)
    cot = to_sequence(cotangent, mine)
    wout = gathered_rows(w_out, mine)
    heads = (jnp.arange(PAD)[:, None] == jnp.arange(E)[None, :] // P_SIZE).astype(bf16)
    heads2 = jnp.concatenate([heads, heads], axis=0)
    hidden, xbc, dt, x, y, starts = forward_call(
        seq, pre, w_xbc, wdt, cw, cb, bias, log_rate, heads2
    )
    normed, d_gate, dy, r1, g_gain, g_skip = gate_call(
        hidden, x, y, cot, w_gate, skip, gain, wout, heads2
    )
    g_out = tn(normed, cot).reshape(2, E // 2, -1)
    g_gate = tn(hidden, d_gate).reshape(2, -1, E)
    early = jnp.concatenate([g_out, g_gate[:, :, : E // 2], g_gate[:, :, E // 2 :]], axis=1)
    early_kept, early_sent = halved(early, mine)
    early_sent, dy = lax.optimization_barrier((early_sent, dy))
    early_come = lax.ppermute(early_sent, "grp", SWAP)
    third = w_in.shape[0]
    result = to_pieces((seq.astype(f32) + nn(normed, wout)).astype(bf16), mine)
    weights = (cw, cb, bias, log_rate, skip, heads2)
    blocks = xbc.shape[0] // BLOCK
    middle = blocks // 2
    high = backward_call(
        middle, blocks, xbc, dt, dy, r1, starts, weights, jnp.zeros((N, E), f32),
        jnp.zeros((8, CH), f32),
    )
    d_state, head, early_come = lax.optimization_barrier((high[6], high[7], early_come))
    early = early_kept + early_come.astype(f32)
    early_kept, early_sent = core_halves(early[None])
    early_sent, d_state = lax.optimization_barrier((early_sent, d_state))
    early_other = flipped(early_sent, 0)
    low = backward_call(0, middle, xbc, dt, dy, r1, starts, weights, d_state, head)
    d_xbc, d_dt = (jnp.concatenate([low[i], high[i]], axis=0) for i in range(2))
    g_cw, g_cb, g_bias, g_log = (low[i] + high[i] for i in range(2, 6))
    late = tn(hidden, d_xbc).reshape(2, -1, CH)
    late_kept, late_sent = core_halves(late)
    late = late_kept + flipped(late_sent, 0).astype(f32)
    late_kept, late_sent = halved(late, mine)
    late = late_kept + lax.ppermute(late_sent, "grp", SWAP).astype(f32)
    late = summed_over_rest(late)
    grad_xbc_w = in_order(late, flipped(late, 0), bit_of(0)).astype(f32)
    early = (early_kept + early_other.astype(f32))[0]
    early = summed_over_rest(early)
    early = in_order(early, flipped(early, 0), bit_of(0)).astype(f32)
    grad_out_w = early[: E // 2]
    grad_gate_w = jnp.concatenate([early[E // 2 : E // 2 + third], early[E // 2 + third :]], axis=1)
    grad_in_w = jnp.concatenate([grad_gate_w, grad_xbc_w], axis=1)
    d_hidden = nt(d_gate, w_gate) + nt(d_xbc, w_xbc) + nt(d_dt, wdt)
    seq32 = seq.astype(f32)
    scale = lax.rsqrt(jnp.mean(seq32 * seq32, axis=-1, keepdims=True) + EPS)
    unit = seq32 * scale
    g_pre = jnp.sum(d_hidden * unit, axis=0)
    d_unit = d_hidden * pre
    d_seq = scale * (d_unit - unit * jnp.mean(d_unit * unit, axis=-1, keepdims=True))
    d_inputs = to_pieces((cot.astype(f32) + d_seq).astype(bf16), mine)
    g_wdt = tn(hidden, d_dt)[:, :H]
    g_skip_h = g_skip.reshape(H, P_SIZE).sum(axis=1)
    small = jnp.concatenate(
        [
            g_wdt.reshape(2, -1), g_pre.reshape(2, -1),
            g_cw.reshape(K, 2, half).transpose(1, 0, 2).reshape(2, -1), g_cb.reshape(2, -1),
            g_gain.reshape(2, -1), g_bias[0, :H].reshape(2, -1), g_log[0, :H].reshape(2, -1),
            g_skip_h.reshape(2, -1),
        ],
        axis=1,
    )
    small = summed_small(small, mine)
    parts, at = [], 0
    for size in (w_dt.size, pre_gain.size, conv_w.size, half, norm_gain.size, 12, 12, 12):
        parts.append(small[at : at + size])
        at += size
    return (
        result, d_inputs, parts[1], grad_in_w, parts[0].reshape(w_dt.shape),
        parts[2].reshape(K, half), parts[3], parts[5], parts[6], parts[7], parts[4], grad_out_w,
    )


def solution(mesh):
    acts, row, mat, taps = P("rep", "grp", None), P("grp"), P("grp", None), P(None, "grp")
    in_specs = (acts, row, mat, mat, taps, row, row, row, row, row, mat, acts)
    out_specs = (acts, acts, row, mat, mat, taps, row, row, row, row, row, mat)
    return jax.shard_map(
        per_device, mesh=mesh, in_specs=in_specs, out_specs=out_specs, check_vma=False
    )
```
